32 devices in a mesh: section: 2 (over core), expert: 16 (over z, y, x).
Axes of the slice: x: 2, y: 2, z: 4, core: 2. Of those that a mesh axis runs over, the one named last changes fastest.
Arguments:
- tokens: bfloat16 [2048, 2048], P('expert'), may hold values from -6 to 6
- cotangent: bfloat16 [2048, 2048], P('expert'), may hold values from -6 to 6
- expert_ids: int32 [2, 2048], P('section', 'expert'), may hold values from 0 to 15, as said below
- up_weight: bfloat16 [2, 16, 2048, 1024], P('section', 'expert'), may hold values from -0.125 to 0.125
- down_weight: bfloat16 [2, 16, 1024, 2048], P('section', 'expert'), may hold values from -0.375 to 0.375
- centroids: float32 [2, 16, 2048], P('section', 'expert'), may hold values from -12 to 12
Outputs:
- acts_out: bfloat16 [2, 2048, 2048], P('section', 'expert')
- grads_in: bfloat16 [2, 2048, 2048], P('section', 'expert')
- centroid_grads: float32 [2, 16, 2048], P('section', 'expert')
The draws below stay inside these ranges and needn't reach their ends.
Inputs may be any that keep to these rules, and one draw needn't show every extreme that they name: `expert_ids`: for each section and each aligned block of 128 rows (the rows of one device), no expert is named by more than 16 rows; in each section one expert is named by exactly 16 rows of every block.
All inputs are finite; a program needn't handle non-finite values.
Results may differ from the reference program's by a relative error of at most 0.0078.
Values may be sent and summed in bfloat16 or wider, within the bound.
No kernel may reach another device: no remote copies, remote signals or barrier semaphores. Data moves between devices by JAX's collectives and lax.ppermute only.
A program may use at most 64 MiB of HBM per device.

```python
import math
import jax
import jax.numpy as jnp
from jax import lax

D = 2048
H = 1024
TOK_DEV = 128
SECTIONS = 2
EXPERTS = 16
TOKENS = 2048
CAP = 16


def draw_expert_ids(key, part):
    key = jax.random.fold_in(key, 11)
    blocks = TOKENS // TOK_DEV

    def one_section(section_key):
        busiest = jax.random.randint(jax.random.fold_in(section_key, 1), (), 0, EXPERTS).astype(jnp.int32)
        labels = (jnp.arange((EXPERTS - 1) * CAP, dtype=jnp.int32) // CAP + busiest + 1) % EXPERTS

        def one_block(block_key):
            pick_key, order_key = jax.random.split(block_key)
            chosen = jax.random.permutation(pick_key, labels)[:TOK_DEV - CAP]
            block_ids = jnp.concatenate([jnp.full((CAP,), busiest, jnp.int32), chosen.astype(jnp.int32)])
            return jax.random.permutation(order_key, block_ids)
        block_keys = jax.random.split(jax.random.fold_in(section_key, 2), blocks)
        return jax.vmap(one_block)(block_keys).reshape(TOKENS)
    return jax.vmap(one_section)(jax.random.split(key, SECTIONS)).astype(jnp.int32)


def block_levels(rng, extent, shards, smallest, largest):
    loudness, own = 1.0, jax.random.fold_in(rng, 6)
    for dim, parts in shards:
        draws = jnp.exp(jax.random.uniform(jax.random.fold_in(own, dim), (parts,), jnp.float32, smallest / len(shards), largest / len(shards)))
        loudness = loudness * jnp.repeat(draws, extent[dim] // parts).reshape([-1 if axis == dim else 1 for axis in range(len(extent))])
    return loudness


def noise(rng, shape, width, bound, shards=(), kind=jnp.bfloat16):
    entries = jax.random.normal(rng, shape, jnp.float32) * width
    if len(shards) > 0:
        entries = block_levels(rng, shape, shards, -0.22, 0.18) * entries
    return jnp.clip(entries, min=-bound, max=bound).astype(kind)


def setup_inputs(seed: int = 0) -> dict:
    seeds = jax.random.split(jax.random.key(seed), 7)
    tokens = noise(seeds[0], (TOKENS, D), 1.0, 6.0, ((0, 16),))
    cotangent = noise(seeds[1], (TOKENS, D), 1.0, 6.0, ((0, 16),))
    expert_ids = draw_expert_ids(jax.random.fold_in(seeds[6], 71), 0)
    up_weight = noise(seeds[3], (SECTIONS, EXPERTS, D, H), D ** -0.5, 0.125, ((0, 2), (1, 16)))
    down_weight = noise(seeds[4], (SECTIONS, EXPERTS, H, D), (H // 4) ** -0.5, 0.375, ((0, 2), (1, 16)))
    centroids = noise(seeds[5], (SECTIONS, EXPERTS, D), 2.0, 12.0, ((0, 2), (1, 16)), jnp.float32)
    return dict(tokens=tokens, cotangent=cotangent, expert_ids=expert_ids, up_weight=up_weight, down_weight=down_weight, centroids=centroids)


def group_rows(expert_of):
    ordering = jnp.argsort(expert_of, stable=True).astype(jnp.int32)
    one_hot = (expert_of[:, None] == jnp.arange(EXPERTS, dtype=jnp.int32)[None, :]).astype(jnp.int32)
    counts = lax.optimization_barrier(jnp.sum(one_hot, axis=0))
    starts = jnp.cumsum(counts) - counts
    slot_ids = jnp.arange(EXPERTS * CAP, dtype=jnp.int32)
    position = jnp.minimum(starts[:, None] + slot_ids[None, :], TOKENS - 1).astype(jnp.int32)
    usable = slot_ids[None, :] < counts[:, None]
    return (ordering[position], usable)

def expert_math(row_data, up_proj, down_proj, centroid, norm_scale):
    preact = jnp.dot(row_data, up_proj, preferred_element_type=jnp.float32)
    hidden = jax.nn.silu(preact).astype(jnp.bfloat16)
    expert_out = jnp.dot(hidden, down_proj, preferred_element_type=jnp.float32)
    logits = lax.optimization_barrier(jnp.sum(row_data.astype(jnp.float32) * centroid[None, :], axis=1)) * norm_scale
    gating = jax.nn.sigmoid(logits)
    return (preact, expert_out, gating)

def expert_grads(row_data, cot_rows, preact, expert_out, gating, up_proj, down_proj, centroid, norm_scale):
    gate_grad = lax.optimization_barrier(jnp.sum(cot_rows.astype(jnp.float32) * expert_out, axis=1))
    logit_grad = gate_grad * gating * (1.0 - gating)
    scaled = (gating[:, None] * cot_rows.astype(jnp.float32)).astype(jnp.bfloat16)
    hidden_grad = jnp.dot(scaled, down_proj.T, preferred_element_type=jnp.float32)
    sigmoid_pre = jax.nn.sigmoid(preact)
    preact_grad = (hidden_grad * sigmoid_pre * (1.0 + preact * (1.0 - sigmoid_pre))).astype(jnp.bfloat16)
    feature_grad = jnp.dot(preact_grad, up_proj.T, preferred_element_type=jnp.float32)
    input_grad = (feature_grad + logit_grad[:, None] * centroid[None, :] * norm_scale).astype(jnp.bfloat16)
    return (input_grad, logit_grad)

def spread_back(per_slot, row_index, usable):
    per_slot = lax.optimization_barrier(per_slot)
    values = jnp.where(usable[:, :, None], per_slot.astype(jnp.float32), 0.0)
    total = jnp.zeros((TOKENS, D), jnp.float32)
    return total.at[row_index.reshape(-1)].add(values.reshape(-1, D))

def layer_forward(layer_in, expert_of, up_proj, down_proj, centroid):
    row_index, usable = group_rows(expert_of)
    norm_scale = 1.0 / math.sqrt(D)

    def per_expert(packed):
        rows_at, usable_at, up_one, down_one, centroid_one = packed
        row_data = jnp.where(usable_at[:, None], layer_in[rows_at], jnp.zeros((), layer_in.dtype))
        preact, expert_out, gating = expert_math(row_data, up_one, down_one, centroid_one, norm_scale)
        return (gating[:, None] * expert_out).astype(jnp.bfloat16)
    branch = lax.map(per_expert, (row_index, usable, up_proj, down_proj, centroid))
    summed = spread_back(branch, row_index, usable)
    return (layer_in.astype(jnp.float32) + summed).astype(jnp.bfloat16)

def layer_backward(layer_in, upstream, expert_of, up_proj, down_proj, centroid):
    row_index, usable = group_rows(expert_of)
    norm_scale = 1.0 / math.sqrt(D)

    def per_expert(packed):
        rows_at, usable_at, up_one, down_one, centroid_one = packed
        row_data = jnp.where(usable_at[:, None], layer_in[rows_at], jnp.zeros((), layer_in.dtype))
        cot_rows = jnp.where(usable_at[:, None], upstream[rows_at], jnp.zeros((), upstream.dtype))
        preact, expert_out, gating = expert_math(row_data, up_one, down_one, centroid_one, norm_scale)
        input_grad, logit_grad = expert_grads(row_data, cot_rows, preact, expert_out, gating, up_one, down_one, centroid_one, norm_scale)
        cent_grad = jnp.dot(logit_grad[None, :], row_data.astype(jnp.float32), precision=lax.Precision.HIGHEST)[0] * norm_scale
        return (input_grad, cent_grad)
    input_grads, cent_grads = lax.map(per_expert, (row_index, usable, up_proj, down_proj, centroid))
    summed = spread_back(input_grads, row_index, usable)
    return ((upstream.astype(jnp.float32) + summed).astype(jnp.bfloat16), cent_grads)

def reference(tokens, cotangent, expert_ids, up_weight, down_weight, centroids):
    acts_one = layer_forward(tokens, expert_ids[0], up_weight[0], down_weight[0], centroids[0])
    acts_two = layer_forward(acts_one, expert_ids[1], up_weight[1], down_weight[1], centroids[1])
    grads_two, cent_two = layer_backward(acts_one, cotangent, expert_ids[1], up_weight[1], down_weight[1], centroids[1])
    grads_one, cent_one = layer_backward(tokens, grads_two, expert_ids[0], up_weight[0], down_weight[0], centroids[0])
    return (jnp.stack([acts_one, acts_two]), jnp.stack([grads_one, grads_two]), jnp.stack([cent_one, cent_two]))
```

```python
import functools
import math

import jax
import jax.numpy as jnp
from jax import lax
from jax.experimental import pallas as pl
from jax.experimental.pallas import tpu as pltpu
from jax.sharding import PartitionSpec as P

BF16 = jnp.bfloat16
F32 = jnp.float32
NN = (((1,), (0,)), ((), ()))
NT = (((1,), (1,)), ((), ()))
TN = (((0,), (0,)), ((), ()))
PARTS = 4


def mul(left, right, dims=NN):
    return lax.dot_general(left, right, dims, preferred_element_type=F32)


def call(body, outs, ins, args, scratch=(), flops=0, moved=0):
    specs = []
    for kind in ins:
        specs.append(
            pl.BlockSpec(
                memory_space={"s": pltpu.SMEM, "v": pltpu.VMEM, "a": pl.ANY}[kind]
            )
        )
    return pl.pallas_call(
        body,
        out_shape=[jax.ShapeDtypeStruct(shape, dtype) for shape, dtype in outs],
        in_specs=specs,
        out_specs=[pl.BlockSpec(memory_space=pltpu.VMEM) for _ in outs],
        scratch_shapes=list(scratch),
        compiler_params=pltpu.CompilerParams(vmem_limit_bytes=40 * 2**20),
        cost_estimate=pl.CostEstimate(flops=flops, bytes_accessed=moved, transcendentals=0),
    )(*args)


def spread_matrix(slot, rows):
    place = lax.broadcasted_iota(jnp.int32, (rows, slot.shape[1]), 0)
    return jnp.where(place == slot, 1.0, 0.0).astype(BF16)


def pick(is_first, first, second):
    return jnp.where(is_first, first, second)


def pack_body(capacity, sec, ids, tokens, cotangent, packed, slot_out):
    count = ids.shape[1]
    across = jnp.broadcast_to(ids[...].astype(F32), (count, count))
    down = across.T
    earlier = lax.broadcasted_iota(jnp.int32, (count, count), 0) < lax.broadcasted_iota(
        jnp.int32, (count, count), 1
    )
    rank = jnp.sum(jnp.where((across == down) & earlier, 1.0, 0.0), axis=0, keepdims=True)
    slot = ids[...] * capacity + rank.astype(jnp.int32)
    slot_out[...] = slot
    spread = spread_matrix(slot, packed.shape[0])

    @pl.when(sec[0] == 0)
    def _():
        packed[...] = mul(spread, tokens[...]).astype(BF16)

    @pl.when(sec[0] != 0)
    def _():
        packed[...] = mul(spread, cotangent[...]).astype(BF16)


def fetch_rows(whole, held, sems):
    step = held.shape[1]
    copies = [
        pltpu.make_async_copy(whole.at[pl.ds(k * step, step), :], held.at[k], sems.at[k])
        for k in range(held.shape[0])
    ]
    for copy in copies:
        copy.start()
    return copies


def fetch_columns(whole, held, sems):
    step = held.shape[2]
    copies = [
        pltpu.make_async_copy(whole.at[:, pl.ds(k * step, step)], held.at[k], sems.at[k])
        for k in range(held.shape[0])
    ]
    for copy in copies:
        copy.start()
    return copies


def gate(rows_parts, centroid, scale):
    total = 0.0
    start = 0
    for rows in rows_parts:
        width = rows.shape[1]
        total = total + jnp.sum(
            rows[...].astype(F32) * centroid[:, start : start + width], axis=1, keepdims=True
        )
        start += width
    return jax.nn.sigmoid(total * scale)


def column(parts, k, step):
    width = parts[0].shape[1]
    at = k * step
    return parts[at // width][:, at % width : at % width + step]


def up_first_body(
    scale, rows, up, down, centroid, keep, send, hidden_out, slope_out, gating_out, up_v, down_v, su, sd
):
    ups = fetch_rows(up, up_v, su)
    downs = fetch_columns(down, down_v, sd)
    gating = gate([rows], centroid, scale)
    gating_out[...] = jnp.broadcast_to(gating, gating_out.shape)
    step = up_v.shape[1]
    preact = 0.0
    for k in range(PARTS):
        ups[k].wait()
        preact = preact + mul(column([rows], k, step), up_v[k])
    sig = jax.nn.sigmoid(preact)
    hidden = (preact * sig).astype(BF16)
    hidden_out[...] = hidden
    slope_out[...] = sig * (1.0 + preact * (1.0 - sig))
    half = PARTS // 2
    step = down_v.shape[2]
    for k in range(PARTS):
        downs[k].wait()
    for k in list(range(half, PARTS)) + list(range(half)):
        branch = (gating * mul(hidden, down_v[k])).astype(BF16)
        target = keep if k < half else send
        target[:, (k % half) * step : (k % half + 1) * step] = branch


def early_body(rows, down, product, down_v, sd):
    downs = fetch_columns(down, down_v, sd)
    step = down_v.shape[2]
    total = 0.0
    for k in range(PARTS):
        downs[k].wait()
        total = total + mul(rows[:, k * step : (k + 1) * step], down_v[k], NT)
    product[...] = total


def second_body(
    scale, low, high, product, up, down, centroid, keep, send, logit_out, up_v, down_v, su, sd
):
    ups = fetch_rows(up, up_v, su)
    downs = fetch_columns(down, down_v, sd)
    gating = gate([low, high], centroid, scale)
    step = up_v.shape[1]
    preact = 0.0
    for k in range(PARTS):
        ups[k].wait()
        preact = preact + mul(column([low, high], k, step), up_v[k])
    sig = jax.nn.sigmoid(preact)
    hidden = (preact * sig).astype(BF16)
    back = product[...]
    logit = jnp.sum(hidden.astype(F32) * back, axis=1, keepdims=True) * gating * (1.0 - gating)
    logit_out[...] = jnp.broadcast_to(logit, logit_out.shape)
    slope = sig * (1.0 + preact * (1.0 - sig))
    pre_grad = (gating * back * slope).astype(BF16)
    half = PARTS // 2
    width = half * step
    for k in range(PARTS):
        target = send if k < half else keep
        at = (k % half) * step
        grad = mul(pre_grad, up_v[k], NT) + logit * (centroid[:, k * step : (k + 1) * step] * scale)
        target[:, at : at + step] = grad.astype(BF16)
    for k in range(PARTS):
        downs[k].wait()
    step = down_v.shape[2]
    for k in range(PARTS):
        target = send if k < half else keep
        at = width + (k % half) * step
        target[:, at : at + step] = (gating * mul(hidden, down_v[k])).astype(BF16)


def first_grads_body(
    scale, low, high, hidden, slope, gating_in, up, down, centroid, keep, send, logit_out,
    up_v, down_v, su, sd,
):
    downs = fetch_columns(down, down_v, sd)
    ups = fetch_rows(up, up_v, su)
    step = down_v.shape[2]
    back = 0.0
    for k in range(PARTS):
        downs[k].wait()
        back = back + mul(column([low, high], k, step), down_v[k], NT)
    gating = gating_in[:, 0:1]
    logit = (
        jnp.sum(hidden[...].astype(F32) * back, axis=1, keepdims=True) * gating * (1.0 - gating)
    )
    logit_out[...] = jnp.broadcast_to(logit, logit_out.shape)
    pre_grad = (gating * back * slope[...]).astype(BF16)
    half = PARTS // 2
    step = up_v.shape[1]
    for k in range(PARTS):
        ups[k].wait()
    for k in list(range(half, PARTS)) + list(range(half)):
        target = keep if k < half else send
        at = (k % half) * step
        grad = mul(pre_grad, up_v[k], NT) + logit * (centroid[:, k * step : (k + 1) * step] * scale)
        target[:, at : at + step] = grad.astype(BF16)


def relay_body(sec, own, other, returned, layer_in, result, packed):
    is_first = sec[0] == 0
    slot_first = pick(is_first, own[...], other[...])
    slot_second = pick(is_first, other[...], own[...])
    rows, width = packed.shape
    mine = pl.ds(pl.multiple_of(sec[0] * width, 128), width)
    branch = mul(spread_matrix(slot_first, rows), returned[...], TN)
    result[...] = (layer_in[:, mine].astype(F32) + branch).astype(BF16)
    packed[...] = mul(spread_matrix(slot_second, rows), result[...]).astype(BF16)


def relay_back_body(sec, own, other, returned, upstream, result, packed):
    is_first = sec[0] == 0
    slot_first = pick(is_first, own[...], other[...])
    slot_second = pick(is_first, other[...], own[...])
    rows, width = packed.shape
    mine = pl.ds(pl.multiple_of(sec[0] * width, 128), width)
    grads = mul(spread_matrix(slot_second, rows), returned[:, :width], TN)
    result[...] = (upstream[:, mine].astype(F32) + grads).astype(BF16)
    packed[...] = mul(spread_matrix(slot_first, rows), result[...]).astype(BF16)


def second_acts_body(sec, own, other, returned, acts_first, stay, leave):
    is_first = sec[0] == 0
    slot_second = pick(is_first, other[...], own[...])
    rows = returned.shape[0]
    width = stay.shape[1]
    branch = mul(spread_matrix(slot_second, rows), returned[:, width:], TN)
    acts_second = (acts_first[...].astype(F32) + branch).astype(BF16)

    @pl.when(is_first)
    def _():
        stay[...] = acts_first[...]
        leave[...] = acts_second

    @pl.when(sec[0] != 0)
    def _():
        stay[...] = acts_second
        leave[...] = acts_first[...]


def join_body(sec, stay, arrived, result):
    width = stay.shape[1]
    result[:, pl.ds(pl.multiple_of(sec[0] * width, 128), width)] = stay[...]
    result[:, pl.ds(pl.multiple_of((1 - sec[0]) * width, 128), width)] = arrived[...]


def finish_body(sec, own, other, low, high, grads_mine, grads_other, result):
    rows, width = low.shape

    @pl.when(sec[0] == 0)
    def _():
        spread = spread_matrix(own[...], rows)
        result[:, :width] = (grads_mine[...].astype(F32) + mul(spread, low[...], TN)).astype(BF16)
        result[:, width:] = (grads_other[...].astype(F32) + mul(spread, high[...], TN)).astype(BF16)

    @pl.when(sec[0] != 0)
    def _():
        result[:, :width] = grads_other[...]
        result[:, width:] = grads_mine[...]


def centroid_body(scale, sec, logit_first, logit_second, rows, low, high, result):
    width = low.shape[1]

    @pl.when(sec[0] == 0)
    def _():
        weight = logit_first[:, 0:1] * scale
        result[...] = jnp.sum(weight * rows[...].astype(F32), axis=0, keepdims=True)

    @pl.when(sec[0] != 0)
    def _():
        weight = logit_second[:, 0:1] * scale
        result[:, :width] = jnp.sum(weight * low[...].astype(F32), axis=0, keepdims=True)
        result[:, width:] = jnp.sum(weight * high[...].astype(F32), axis=0, keepdims=True)


def swap(value):
    return lax.ppermute(value, "section", [(0, 1), (1, 0)])


def exchange(value):
    return lax.all_to_all(value, "expert", split_axis=0, concat_axis=0, tiled=True)


def shards(tokens, cotangent, expert_ids, up_weight, down_weight, centroids):
    experts = lax.axis_size("expert")
    count, width = tokens.shape
    hidden_width = up_weight.shape[3]
    half = width // 2
    capacity = 2 * count // experts
    rows = experts * capacity
    scale = 1.0 / math.sqrt(width)
    up = up_weight.reshape(width, hidden_width)
    down = down_weight.reshape(hidden_width, width)
    centroid = centroids.reshape(1, width)
    section = lax.axis_index("section")
    is_first = section == 0
    sec = section.astype(jnp.int32).reshape(1)

    up_scratch = pltpu.VMEM((PARTS, width // PARTS, hidden_width), BF16)
    down_scratch = pltpu.VMEM((PARTS, hidden_width, width // PARTS), BF16)
    sems = pltpu.SemaphoreType.DMA((PARTS,))
    weights = width * hidden_width
    product = 2 * rows * weights

    packed, own = call(
        functools.partial(pack_body, capacity),
        [((rows, width), BF16), ((1, count), jnp.int32)],
        "svvv",
        (sec, expert_ids, tokens, cotangent),
        flops=2 * rows * count * width,
        moved=4 * rows * width,
    )
    received = exchange(packed)
    other = swap(own)

    keep, send, hidden, slope, gating = call(
        functools.partial(up_first_body, scale),
        [
            ((rows, half), BF16),
            ((rows, half), BF16),
            ((rows, hidden_width), BF16),
            ((rows, hidden_width), F32),
            ((rows, 128), F32),
        ],
        "vaav",
        (received, up, down, centroid),
        (up_scratch, down_scratch, sems, sems),
        flops=2 * product,
        moved=4 * weights + 10 * rows * width // 2,
    )
    returned = exchange(jnp.where(is_first, keep, swap(send)))
    (back_early,) = call(
        early_body,
        [((rows, hidden_width), F32)],
        "va",
        (received, down),
        (down_scratch, sems),
        flops=product,
        moved=2 * weights + 4 * rows * width,
    )
    acts_first, packed = call(
        relay_body,
        [((count, half), BF16), ((rows, half), BF16)],
        "svvvv",
        (sec, own, other, returned, tokens),
        flops=4 * rows * count * half,
        moved=4 * rows * half + 4 * count * width,
    )

    mine = exchange(packed)
    theirs = swap(mine)
    low, high = theirs, mine
    keep, send, logit_second = call(
        functools.partial(second_body, scale),
        [((rows, width), BF16), ((rows, width), BF16), ((rows, 128), F32)],
        "vvvaav",
        (low, high, back_early, up, down, centroid),
        (up_scratch, down_scratch, sems, sems),
        flops=3 * product,
        moved=4 * weights + 10 * rows * width,
    )
    returned = exchange(jnp.where(is_first, swap(send), keep))
    grads_second, packed = call(
        relay_back_body,
        [((count, half), BF16), ((rows, half), BF16)],
        "svvvv",
        (sec, own, other, returned, cotangent),
        flops=4 * rows * count * half,
        moved=4 * rows * half + 4 * count * width,
    )

    mine = exchange(packed)
    stay, leave = call(
        second_acts_body,
        [((count, half), BF16), ((count, half), BF16)],
        "svvvv",
        (sec, own, other, returned, acts_first),
        flops=2 * rows * count * half,
        moved=2 * rows * width + 6 * count * half,
    )
    (acts,) = call(
        join_body, [((count, width), BF16)], "svv", (sec, stay, swap(leave)), moved=4 * count * width
    )
    grads_other = swap(grads_second)
    theirs = swap(mine)
    keep, send, logit_first = call(
        functools.partial(first_grads_body, scale),
        [((rows, half), BF16), ((rows, half), BF16), ((rows, 128), F32)],
        "vvvvvaav",
        (mine, theirs, hidden, slope, gating, up, down, centroid),
        (up_scratch, down_scratch, sems, sems),
        flops=2 * product,
        moved=4 * weights + 10 * rows * width,
    )
    mine = exchange(jnp.where(is_first, keep, swap(send)))
    (cent_grad,) = call(
        functools.partial(centroid_body, scale),
        [((1, width), F32)],
        "svvvvv",
        (sec, logit_first, logit_second, received, low, high),
        flops=4 * rows * width,
        moved=6 * rows * width,
    )
    (grads,) = call(
        finish_body,
        [((count, width), BF16)],
        "svvvvvv",
        (sec, own, other, mine, swap(mine), grads_second, grads_other),
        flops=2 * rows * count * width,
        moved=4 * rows * width,
    )
    return (acts[None], grads[None], cent_grad[None])


def solution(mesh):
    return jax.shard_map(
        shards,
        mesh=mesh,
        in_specs=(
            P("expert", None),
            P("expert", None),
            P("section", "expert"),
            P("section", "expert", None, None),
            P("section", "expert", None, None),
            P("section", "expert", None),
        ),
        out_specs=(
            P("section", "expert", None),
            P("section", "expert", None),
            P("section", "expert", None),
        ),
        check_vma=False,
    )
```

```python
import functools
import math

import jax
import jax.numpy as jnp
from jax import lax
from jax.experimental import pallas as pl
from jax.experimental.pallas import tpu as pltpu
from jax.sharding import PartitionSpec as P

BF16 = jnp.bfloat16
F32 = jnp.float32
NN = (((1,), (0,)), ((), ()))
NT = (((1,), (1,)), ((), ()))
TN = (((0,), (0,)), ((), ()))
PARTS = 4


def mul(left, right, dims=NN):
    return lax.dot_general(left, right, dims, preferred_element_type=F32)


def call(body, outs, ins, args, scratch=(), flops=0, moved=0, grant=16):
    specs = []
    for kind in ins:
        specs.append(
            pl.BlockSpec(
                memory_space={"s": pltpu.SMEM, "v": pltpu.VMEM, "h": pltpu.HBM}[kind]
            )
        )
    return pl.pallas_call(
        body,
        out_shape=[jax.ShapeDtypeStruct(shape, dtype) for shape, dtype in outs],
        in_specs=specs,
        out_specs=[pl.BlockSpec(memory_space=pltpu.VMEM) for _ in outs],
        scratch_shapes=list(scratch),
        compiler_params=pltpu.CompilerParams(vmem_limit_bytes=grant * 2**20),
        cost_estimate=pl.CostEstimate(flops=flops, bytes_accessed=moved, transcendentals=0),
    )(*args)


def spread_matrix(slot, rows):
    place = lax.broadcasted_iota(jnp.int32, (rows, slot.shape[1]), 0)
    return jnp.where(place == slot, 1.0, 0.0).astype(BF16)


def pick(is_first, first, second):
    return jnp.where(is_first, first, second)


def blocks(total, parts):
    step = total // parts
    return [slice(k * step, (k + 1) * step) for k in range(parts)]


def pack_body(capacity, sec, ids_in, tokens, cotangent, packed, slot_out, ids, rows, sems):
    ids_copy = pltpu.make_async_copy(ids_in, ids, sems.at[0])
    ids_copy.start()

    @pl.when(sec[0] == 0)
    def _():
        pltpu.make_async_copy(tokens, rows, sems.at[1]).start()

    @pl.when(sec[0] != 0)
    def _():
        pltpu.make_async_copy(cotangent, rows, sems.at[1]).start()

    ids_copy.wait()
    count = ids.shape[1]
    across = jnp.broadcast_to(ids[...].astype(F32), (count, count))
    down = across.T
    earlier = lax.broadcasted_iota(jnp.int32, (count, count), 0) < lax.broadcasted_iota(
        jnp.int32, (count, count), 1
    )
    rank = jnp.sum(jnp.where((across == down) & earlier, 1.0, 0.0), axis=0, keepdims=True)
    slot = ids[...] * capacity + rank.astype(jnp.int32)
    slot_out[...] = slot
    spread = spread_matrix(slot, packed.shape[0])
    pltpu.make_async_copy(tokens, rows, sems.at[1]).wait()
    packed[...] = mul(spread, rows[...]).astype(BF16)


def gate(row_parts, centroid, scale):
    total = 0.0
    start = 0
    for rows in row_parts:
        width = rows.shape[1]
        for at in blocks(width, 4):
            total = total + jnp.sum(
                rows[:, at].astype(F32) * centroid[:, start + at.start : start + at.stop],
                axis=1,
                keepdims=True,
            )
        start += width
    return jax.nn.sigmoid(total * scale)


def back_through(low_parts, down, at):
    total = 0.0
    start = 0
    for rows in low_parts:
        width = rows.shape[1]
        total = total + mul(rows[...], down[at, start : start + width], NT)
        start += width
    return total


def up_first_body(
    scale, sec, rows, up, down, centroid, keep, send, hidden, aux, gating_out
):
    half = keep.shape[1]

    @pl.when(sec[0] == 0)
    def _():
        gating = gate([rows], centroid, scale)
        gating_out[...] = jnp.broadcast_to(gating, gating_out.shape)
        for at in blocks(up.shape[1], PARTS):
            preact = mul(rows[...], up[:, at])
            sig = jax.nn.sigmoid(preact)
            hidden[:, at] = (preact * sig).astype(BF16)
            aux[:, at] = sig * (1.0 + preact * (1.0 - sig))
        for at in blocks(down.shape[1], PARTS):
            target = keep if at.start < half else send
            into = slice(at.start % half, at.start % half + at.stop - at.start)
            target[:, into] = (gating * mul(hidden[...], down[:, at])).astype(BF16)

    @pl.when(sec[0] != 0)
    def _():
        for at in blocks(down.shape[0], PARTS):
            aux[:, at] = back_through([rows], down, at)


def second_body(
    scale, sec, low, high, back, up, down, centroid, keep, send, logit_out, hidden, pre_grad
):
    half = low.shape[1]

    @pl.when(sec[0] != 0)
    def _():
        gating = gate([low, high], centroid, scale)
        total = 0.0
        for at in blocks(up.shape[1], PARTS):
            preact = mul(low[...], up[:half, at]) + mul(high[...], up[half:, at])
            sig = jax.nn.sigmoid(preact)
            hidden_part = (preact * sig).astype(BF16)
            hidden[:, at] = hidden_part
            back_part = back[:, at]
            total = total + jnp.sum(hidden_part.astype(F32) * back_part, axis=1, keepdims=True)
            slope = sig * (1.0 + preact * (1.0 - sig))
            pre_grad[:, at] = (gating * back_part * slope).astype(BF16)
        logit = total * gating * (1.0 - gating)
        logit_out[...] = jnp.broadcast_to(logit, logit_out.shape)
        for at in blocks(down.shape[1], PARTS):
            target = send if at.start < half else keep
            into = slice(at.start % half, at.start % half + at.stop - at.start)
            grad = mul(pre_grad[...], up[at, :], NT) + logit * (centroid[:, at] * scale)
            target[:, into] = grad.astype(BF16)
            target[:, half + into.start : half + into.stop] = (
                gating * mul(hidden[...], down[:, at])
            ).astype(BF16)


def first_grads_body(
    scale, sec, low, high, hidden, slope, gating_in, mark, up, down, centroid, keep, send,
    logit_out, pre_grad,
):
    half = low.shape[1]

    @pl.when(sec[0] == 0)
    def _():
        gating = gating_in[:, 0:1]
        total = 0.0
        for at in blocks(down.shape[0], PARTS):
            back_part = back_through([low, high], down, at)
            total = total + jnp.sum(
                hidden[:, at].astype(F32) * back_part, axis=1, keepdims=True
            )
            pre_grad[:, at] = (gating * back_part * slope[:, at]).astype(BF16)
        logit = total * gating * (1.0 - gating)
        logit_out[...] = jnp.broadcast_to(logit, logit_out.shape)
        for at in blocks(up.shape[0], PARTS):
            target = keep if at.start < half else send
            into = slice(at.start % half, at.start % half + at.stop - at.start)
            grad = mul(pre_grad[...], up[at, :], NT) + logit * (centroid[:, at] * scale)
            target[:, into] = grad.astype(BF16)


def relay_body(sec, own, other, returned, layer_in, result, packed):
    is_first = sec[0] == 0
    slot_first = pick(is_first, own[...], other[...])
    slot_second = pick(is_first, other[...], own[...])
    rows, width = packed.shape
    mine = pl.ds(pl.multiple_of(sec[0] * width, 128), width)
    branch = mul(spread_matrix(slot_first, rows), returned[...], TN)
    result[...] = (layer_in[:, mine].astype(F32) + branch).astype(BF16)
    packed[...] = mul(spread_matrix(slot_second, rows), result[...]).astype(BF16)


def relay_back_body(sec, own, other, returned, upstream, result, packed):
    is_first = sec[0] == 0
    slot_first = pick(is_first, own[...], other[...])
    slot_second = pick(is_first, other[...], own[...])
    rows, width = packed.shape
    mine = pl.ds(pl.multiple_of(sec[0] * width, 128), width)
    grads = mul(spread_matrix(slot_second, rows), returned[:, :width], TN)
    result[...] = (upstream[:, mine].astype(F32) + grads).astype(BF16)
    packed[...] = mul(spread_matrix(slot_first, rows), result[...]).astype(BF16)


def second_acts_body(sec, own, other, returned, acts_first, stay, leave):
    is_first = sec[0] == 0
    slot_second = pick(is_first, other[...], own[...])
    rows = returned.shape[0]
    width = stay.shape[1]
    branch = mul(spread_matrix(slot_second, rows), returned[:, width:], TN)
    acts_second = (acts_first[...].astype(F32) + branch).astype(BF16)

    @pl.when(is_first)
    def _():
        stay[...] = acts_first[...]
        leave[...] = acts_second

    @pl.when(sec[0] != 0)
    def _():
        stay[...] = acts_second
        leave[...] = acts_first[...]


def join_body(sec, stay, arrived, result, mark):
    width = stay.shape[1]
    result[:, pl.ds(pl.multiple_of(sec[0] * width, 128), width)] = stay[...]
    result[:, pl.ds(pl.multiple_of((1 - sec[0]) * width, 128), width)] = arrived[...]
    mark[...] = jnp.zeros_like(mark)


def finish_body(sec, own, other, low, high, grads_mine, grads_other, cent, result):
    rows, width = low.shape

    @pl.when(sec[0] == 0)
    def _():
        spread = spread_matrix(own[...], rows)
        result[:, :width] = (grads_mine[...].astype(F32) + mul(spread, low[...], TN)).astype(BF16)
        result[:, width:] = (grads_other[...].astype(F32) + mul(spread, high[...], TN)).astype(BF16)

    @pl.when(sec[0] != 0)
    def _():
        result[:, :width] = grads_other[...]
        result[:, width:] = grads_mine[...]


def centroid_body(scale, sec, logit_first, logit_second, rows, low, high, result):
    width = low.shape[1]

    @pl.when(sec[0] == 0)
    def _():
        weight = logit_first[:, 0:1] * scale
        result[...] = jnp.sum(weight * rows[...].astype(F32), axis=0, keepdims=True)

    @pl.when(sec[0] != 0)
    def _():
        weight = logit_second[:, 0:1] * scale
        result[:, :width] = jnp.sum(weight * low[...].astype(F32), axis=0, keepdims=True)
        result[:, width:] = jnp.sum(weight * high[...].astype(F32), axis=0, keepdims=True)


def swap(value):
    return lax.ppermute(value, "section", [(0, 1), (1, 0)])


def exchange(value):
    return lax.all_to_all(value, "expert", split_axis=0, concat_axis=0, tiled=True)


def shards(tokens, cotangent, expert_ids, up_weight, down_weight, centroids):
    experts = lax.axis_size("expert")
    count, width = tokens.shape
    hidden_width = up_weight.shape[3]
    half = width // 2
    capacity = 2 * count // experts
    rows = experts * capacity
    scale = 1.0 / math.sqrt(width)
    up = up_weight.reshape(width, hidden_width)
    down = down_weight.reshape(hidden_width, width)
    centroid = centroids.reshape(1, width)
    section = lax.axis_index("section")
    is_first = section == 0
    sec = section.astype(jnp.int32).reshape(1)

    product = 2 * rows * width * hidden_width

    packed, own = call(
        functools.partial(pack_body, capacity),
        [((rows, width), BF16), ((1, count), jnp.int32)],
        "shhh",
        (sec, expert_ids, tokens, cotangent),
        (
            pltpu.VMEM((1, count), jnp.int32),
            pltpu.VMEM((count, width), BF16),
            pltpu.SemaphoreType.DMA((2,)),
        ),
        flops=100 * product,
        moved=4 * rows * width,
    )
    received = exchange(packed)
    other = swap(own)
    keep, send, hidden, aux, gating = call(
        functools.partial(up_first_body, scale),
        [
            ((rows, half), BF16),
            ((rows, half), BF16),
            ((rows, hidden_width), BF16),
            ((rows, hidden_width), F32),
            ((rows, 128), F32),
        ],
        "svvvv",
        (sec, received, up, down, centroid),
        flops=2 * product,
        moved=10 * rows * width,
    )
    returned = exchange(jnp.where(is_first & (other[0, 0] >= 0), keep, swap(send)))
    acts_first, packed = call(
        relay_body,
        [((count, half), BF16), ((rows, half), BF16)],
        "svvvv",
        (sec, own, other, returned, tokens),
        flops=100 * product,
        moved=4 * rows * half + 4 * count * width,
    )

    mine = exchange(packed)
    theirs = swap(mine)
    low, high = theirs, mine
    keep, send, logit_second = call(
        functools.partial(second_body, scale),
        [((rows, width), BF16), ((rows, width), BF16), ((rows, 128), F32)],
        "svvvvvv",
        (sec, low, high, aux, up, down, centroid),
        (pltpu.VMEM((rows, hidden_width), BF16), pltpu.VMEM((rows, hidden_width), BF16)),
        flops=3 * product,
        moved=10 * rows * width,
    )
    returned = exchange(jnp.where(is_first, swap(send), keep))
    grads_second, packed = call(
        relay_back_body,
        [((count, half), BF16), ((rows, half), BF16)],
        "svvvv",
        (sec, own, other, returned, cotangent),
        flops=100 * product,
        moved=4 * rows * half + 4 * count * width,
    )

    mine = exchange(packed)
    stay, leave = call(
        second_acts_body,
        [((count, half), BF16), ((count, half), BF16)],
        "svvvv",
        (sec, own, other, returned, acts_first),
        flops=2 * rows * count * half,
        moved=2 * rows * width + 6 * count * half,
    )
    acts, mark = call(
        join_body,
        [((count, width), BF16), ((8, 128), F32)],
        "svv",
        (sec, stay, swap(leave)),
        moved=4 * count * width,
    )
    grads_other = swap(grads_second)
    theirs = swap(mine)
    keep, send, logit_first = call(
        functools.partial(first_grads_body, scale),
        [((rows, half), BF16), ((rows, half), BF16), ((rows, 128), F32)],
        "svvvvvvvvv",
        (sec, mine, theirs, hidden, aux, gating, mark, up, down, centroid),
        (pltpu.VMEM((rows, hidden_width), BF16),),
        flops=2 * product,
        moved=10 * rows * width,
    )
    mine = exchange(jnp.where(is_first, keep, swap(send)))
    (cent_grad,) = call(
        functools.partial(centroid_body, scale),
        [((1, width), F32)],
        "svvvvv",
        (sec, logit_first, logit_second, received, low, high),
        flops=4 * rows * width,
        moved=6 * rows * width,
    )
    (grads,) = call(
        finish_body,
        [((count, width), BF16)],
        "svvvvvvv",
        (sec, own, other, mine, swap(mine), grads_second, grads_other, cent_grad),
        flops=2 * rows * count * width,
        moved=4 * rows * width,
    )
    return (acts[None], grads[None], cent_grad[None])


def solution(mesh):
    return jax.shard_map(
        shards,
        mesh=mesh,
        in_specs=(
            P("expert", None),
            P("expert", None),
            P("section", "expert"),
            P("section", "expert", None, None),
            P("section", "expert", None, None),
            P("section", "expert", None),
        ),
        out_specs=(
            P("section", "expert", None),
            P("section", "expert", None),
            P("section", "expert", None),
        ),
        check_vma=False,
    )
```

```python
import functools
import math

import jax
import jax.numpy as jnp
from jax import lax
from jax.experimental import pallas as pl
from jax.experimental.pallas import tpu as pltpu
from jax.sharding import PartitionSpec as P

BF16 = jnp.bfloat16
F32 = jnp.float32
NN = (((1,), (0,)), ((), ()))
NT = (((1,), (1,)), ((), ()))
TN = (((0,), (0,)), ((), ()))
PARTS = 4


def mul(left, right, dims=NN):
    return lax.dot_general(left, right, dims, preferred_element_type=F32)


def call(body, outs, ins, args, scratch=(), flops=0, moved=0, grant=16):
    specs = []
    for kind in ins:
        specs.append(
            pl.BlockSpec(
                memory_space={"s": pltpu.SMEM, "v": pltpu.VMEM, "h": pltpu.HBM}[kind]
            )
        )
    return pl.pallas_call(
        body,
        out_shape=[jax.ShapeDtypeStruct(shape, dtype) for shape, dtype in outs],
        in_specs=specs,
        out_specs=[pl.BlockSpec(memory_space=pltpu.VMEM) for _ in outs],
        scratch_shapes=list(scratch),
        compiler_params=pltpu.CompilerParams(vmem_limit_bytes=grant * 2**20),
        cost_estimate=pl.CostEstimate(flops=flops, bytes_accessed=moved, transcendentals=0),
    )(*args)


def spread_matrix(slot, rows):
    place = lax.broadcasted_iota(jnp.int32, (rows, slot.shape[1]), 0)
    return jnp.where(place == slot, 1.0, 0.0).astype(BF16)


def pick(is_first, first, second):
    return jnp.where(is_first, first, second)


def blocks(total, parts):
    step = total // parts
    return [slice(k * step, (k + 1) * step) for k in range(parts)]


def pack_body(capacity, ids, rows, packed, slot_out):
    count = ids.shape[1]
    across = jnp.broadcast_to(ids[...].astype(F32), (count, count))
    down = across.T
    earlier = lax.broadcasted_iota(jnp.int32, (count, count), 0) < lax.broadcasted_iota(
        jnp.int32, (count, count), 1
    )
    rank = jnp.sum(jnp.where((across == down) & earlier, 1.0, 0.0), axis=0, keepdims=True)
    slot = ids[...] * capacity + rank.astype(jnp.int32)
    slot_out[...] = slot
    packed[...] = mul(spread_matrix(slot, packed.shape[0]), rows[...]).astype(BF16)


def gate_sum(rows, centroid, start):
    total = 0.0
    for at in blocks(rows.shape[1], 4):
        total = total + jnp.sum(
            rows[:, at].astype(F32) * centroid[:, start + at.start : start + at.stop],
            axis=1,
            keepdims=True,
        )
    return total


def spread_column(values, ref):
    ref[...] = jnp.broadcast_to(values, ref.shape)


def first_body(scale, sec, rows, up, down, centroid, send, keep, hidden, aux, gating_out):
    half = send.shape[1]

    @pl.when(sec[0] == 0)
    def _():
        gating = jax.nn.sigmoid(gate_sum(rows, centroid, 0) * scale)
        spread_column(gating, gating_out)
        for at in blocks(up.shape[1], PARTS):
            preact = mul(rows[...], up[:, at])
            sig = jax.nn.sigmoid(preact)
            hidden[:, at] = (preact * sig).astype(BF16)
            aux[:, at] = sig * (1.0 + preact * (1.0 - sig))
        for target, start in ((send, half), (keep, 0)):
            for at in blocks(half, 2):
                into = slice(start + at.start, start + at.stop)
                target[:, at] = (gating * mul(hidden[...], down[:, into])).astype(BF16)

    @pl.when(sec[0] != 0)
    def _():
        for at in blocks(down.shape[0], PARTS):
            aux[:, at] = mul(rows[...], down[at, :], NT)


def choose_body(sec, keep, arrived, other, result):
    @pl.when(sec[0] == 0)
    def _():
        result[...] = keep[...]

    @pl.when(sec[0] != 0)
    def _():
        result[...] = arrived[...]


def second_ahead_body(sec, high, up, centroid, preact, gate_out):
    half = high.shape[1]

    @pl.when(sec[0] != 0)
    def _():
        spread_column(gate_sum(high, centroid, half), gate_out)
        for at in blocks(up.shape[1], PARTS):
            preact[:, at] = mul(high[...], up[half:, at])


def section_results(scale, target, start, pre_grad, hidden, logit, gating, up, down, centroid):
    half = target.shape[1] // 2
    for at in blocks(half, 2):
        into = slice(start + at.start, start + at.stop)
        grad = mul(pre_grad[...], up[into, :], NT) + logit * (centroid[:, into] * scale)
        target[:, at] = grad.astype(BF16)
        target[:, half + at.start : half + at.stop] = (
            gating * mul(hidden[...], down[:, into])
        ).astype(BF16)


def second_body(
    scale, sec, low, ahead, gate_ahead, back, up, down, centroid,
    send, logit_out, hidden, pre_grad, gating_out,
):
    half = low.shape[1]

    @pl.when(sec[0] != 0)
    def _():
        gating = jax.nn.sigmoid((gate_sum(low, centroid, 0) + gate_ahead[:, 0:1]) * scale)
        spread_column(gating, gating_out)
        total = 0.0
        for at in blocks(up.shape[1], PARTS):
            preact = mul(low[...], up[:half, at]) + ahead[:, at]
            sig = jax.nn.sigmoid(preact)
            hidden_part = (preact * sig).astype(BF16)
            hidden[:, at] = hidden_part
            back_part = back[:, at]
            total = total + jnp.sum(hidden_part.astype(F32) * back_part, axis=1, keepdims=True)
            slope = sig * (1.0 + preact * (1.0 - sig))
            pre_grad[:, at] = (gating * back_part * slope).astype(BF16)
        logit = total * gating * (1.0 - gating)
        spread_column(logit, logit_out)
        section_results(scale, send, 0, pre_grad, hidden, logit, gating, up, down, centroid)


def second_stay_body(
    scale, sec, logit, hidden, pre_grad, gating, up, down, centroid, keep
):
    half = keep.shape[1] // 2

    @pl.when(sec[0] != 0)
    def _():
        section_results(
            scale, keep, half, pre_grad, hidden, logit[:, 0:1], gating[:, 0:1], up, down, centroid
        )


def grads_ahead_body(sec, low, down, back):
    half = low.shape[1]

    @pl.when(sec[0] == 0)
    def _():
        for at in blocks(down.shape[0], PARTS):
            back[:, at] = mul(low[...], down[at, :half], NT)


def first_grads_body(
    scale, sec, high, ahead, hidden, slope, gating_in, up, down, centroid, leave, grads_other,
    send, logit_out, pre_grad,
):
    half = high.shape[1]

    @pl.when(sec[0] == 0)
    def _():
        gating = gating_in[:, 0:1]
        total = 0.0
        for at in blocks(down.shape[0], PARTS):
            back = mul(high[...], down[at, half:], NT) + ahead[:, at]
            total = total + jnp.sum(hidden[:, at].astype(F32) * back, axis=1, keepdims=True)
            pre_grad[:, at] = (gating * back * slope[:, at]).astype(BF16)
        logit = total * gating * (1.0 - gating)
        spread_column(logit, logit_out)
        input_grads(scale, send, half, pre_grad, logit, up, centroid)


def input_grads(scale, target, start, pre_grad, logit, up, centroid):
    for at in blocks(target.shape[1], 2):
        into = slice(start + at.start, start + at.stop)
        grad = mul(pre_grad[...], up[into, :], NT) + logit * (centroid[:, into] * scale)
        target[:, at] = grad.astype(BF16)


def first_grads_stay_body(scale, sec, logit, pre_grad, up, centroid, keep):
    @pl.when(sec[0] == 0)
    def _():
        input_grads(scale, keep, 0, pre_grad, logit[:, 0:1], up, centroid)


def relay_body(sec, own, other, returned, layer_in, result, packed):
    is_first = sec[0] == 0
    slot_first = pick(is_first, own[...], other[...])
    slot_second = pick(is_first, other[...], own[...])
    rows, width = packed.shape
    mine = pl.ds(pl.multiple_of(sec[0] * width, 128), width)
    branch = mul(spread_matrix(slot_first, rows), returned[...], TN)
    result[...] = (layer_in[:, mine].astype(F32) + branch).astype(BF16)
    packed[...] = mul(spread_matrix(slot_second, rows), result[...]).astype(BF16)


def relay_back_body(
    sec, own, other, returned, upstream, acts_first, result, packed, stay, leave
):
    is_first = sec[0] == 0
    slot_first = pick(is_first, own[...], other[...])
    slot_second = pick(is_first, other[...], own[...])
    rows, width = packed.shape
    mine = pl.ds(pl.multiple_of(sec[0] * width, 128), width)
    spread = spread_matrix(slot_second, rows)
    grads = mul(spread, returned[:, :width], TN)
    result[...] = (upstream[:, mine].astype(F32) + grads).astype(BF16)
    packed[...] = mul(spread_matrix(slot_first, rows), result[...]).astype(BF16)
    branch = mul(spread, returned[:, width:], TN)
    acts_second = (acts_first[...].astype(F32) + branch).astype(BF16)

    @pl.when(is_first)
    def _():
        stay[...] = acts_first[...]
        leave[...] = acts_second

    @pl.when(sec[0] != 0)
    def _():
        stay[...] = acts_second
        leave[...] = acts_first[...]


def join_body(sec, stay, arrived, result, mark):
    width = stay.shape[1]
    result[:, pl.ds(pl.multiple_of(sec[0] * width, 128), width)] = stay[...]
    result[:, pl.ds(pl.multiple_of((1 - sec[0]) * width, 128), width)] = arrived[...]
    mark[...] = jnp.zeros_like(mark)


def finish_body(sec, own, other, low, high, grads_mine, grads_other, mark, late, result):
    rows, width = low.shape

    @pl.when(sec[0] == 0)
    def _():
        spread = spread_matrix(own[...], rows)
        result[:, :width] = (grads_mine[...].astype(F32) + mul(spread, low[...], TN)).astype(BF16)
        result[:, width:] = (grads_other[...].astype(F32) + mul(spread, high[...], TN)).astype(BF16)

    @pl.when(sec[0] != 0)
    def _():
        result[:, :width] = grads_other[...]
        result[:, width:] = grads_mine[...]


def centroid_body(scale, sec, logit_first, logit_second, rows, low, high, result, mark):
    mark[...] = jnp.zeros_like(mark)
    width = low.shape[1]

    @pl.when(sec[0] == 0)
    def _():
        weight = logit_first[:, 0:1] * scale
        result[...] = jnp.sum(weight * rows[...].astype(F32), axis=0, keepdims=True)

    @pl.when(sec[0] != 0)
    def _():
        weight = logit_second[:, 0:1] * scale
        result[:, :width] = jnp.sum(weight * low[...].astype(F32), axis=0, keepdims=True)
        result[:, width:] = jnp.sum(weight * high[...].astype(F32), axis=0, keepdims=True)


def swap(value):
    return lax.ppermute(value, "section", [(0, 1), (1, 0)])


def exchange(value):
    return lax.all_to_all(value, "expert", split_axis=0, concat_axis=0, tiled=True)


def shards(tokens, cotangent, expert_ids, up_weight, down_weight, centroids):
    experts = lax.axis_size("expert")
    count, width = tokens.shape
    hidden_width = up_weight.shape[3]
    half = width // 2
    capacity = 2 * count // experts
    rows = experts * capacity
    scale = 1.0 / math.sqrt(width)
    up = up_weight.reshape(width, hidden_width)
    down = down_weight.reshape(hidden_width, width)
    centroid = centroids.reshape(1, width)
    section = lax.axis_index("section")
    is_first = section == 0
    sec = section.astype(jnp.int32).reshape(1)

    product = 2 * rows * width * hidden_width

    wide, tall, thin = ((rows, width), BF16), ((rows, hidden_width), BF16), ((rows, 128), F32)
    narrow, deep = ((rows, half), BF16), ((rows, hidden_width), F32)
    home, mark_shape = ((count, half), BF16), ((8, 128), F32)

    packed, own = call(
        functools.partial(pack_body, capacity),
        [wide, ((1, count), jnp.int32)],
        "vv",
        (expert_ids, jnp.where(is_first, tokens, cotangent)),
        flops=100 * product,
        moved=4 * rows * width,
    )
    received = exchange(packed)
    other = swap(own)

    send, keep, hidden, aux, gating = call(
        functools.partial(first_body, scale),
        [narrow, narrow, tall, deep, thin],
        "svvvv",
        (sec, received, up, down, centroid),
        flops=2 * product,
        moved=10 * rows * width,
    )
    (chosen,) = call(
        choose_body, [narrow], "svvv", (sec, keep, swap(send), other), flops=100 * product
    )
    returned = exchange(chosen)
    acts_first, packed = call(
        relay_body,
        [home, narrow],
        "svvvv",
        (sec, own, other, returned, tokens),
        flops=100 * product,
        moved=4 * rows * half + 4 * count * width,
    )

    high = exchange(packed)
    low = swap(high)
    ahead, gate_ahead = call(
        second_ahead_body,
        [deep, thin],
        "svvv",
        (sec, high, up, centroid),
        flops=product // 2,
        moved=4 * rows * width,
    )
    send, logit_second, hidden_second, pre_grad, gating_second = call(
        functools.partial(second_body, scale),
        [wide, thin, tall, tall, thin],
        "svvvvvvv",
        (sec, low, ahead, gate_ahead, aux, up, down, centroid),
        flops=2 * product,
        moved=10 * rows * width,
    )
    (keep,) = call(
        functools.partial(second_stay_body, scale),
        [wide],
        "svvvvvvv",
        (sec, logit_second, hidden_second, pre_grad, gating_second, up, down, centroid),
        flops=product,
        moved=6 * rows * width,
    )
    returned = exchange(jnp.where(is_first, swap(send), keep))
    grads_second, packed, stay, leave = call(
        relay_back_body,
        [home, narrow, home, home],
        "svvvvv",
        (sec, own, other, returned, cotangent, acts_first),
        flops=100 * product,
        moved=4 * rows * half + 4 * count * width,
    )

    mine = exchange(packed)
    theirs = swap(mine)
    grads_other = swap(grads_second)
    arrived = swap(leave)
    (ahead,) = call(
        grads_ahead_body,
        [deep],
        "svv",
        (sec, mine, down),
        flops=product // 2,
        moved=4 * rows * width,
    )
    send, logit_first, pre_grad = call(
        functools.partial(first_grads_body, scale),
        [narrow, thin, tall],
        "svvvvvvvvvv",
        (sec, theirs, ahead, hidden, aux, gating, up, down, centroid, arrived, grads_other),
        flops=2 * product,
        moved=10 * rows * width,
    )
    (keep,) = call(
        functools.partial(first_grads_stay_body, scale),
        [narrow],
        "svvvv",
        (sec, logit_first, pre_grad, up, centroid),
        flops=product // 2,
        moved=4 * rows * width,
    )
    mine = exchange(jnp.where(is_first, keep, swap(send)))
    acts, mark = call(
        join_body,
        [((count, width), BF16), mark_shape],
        "svv",
        (sec, stay, arrived),
        moved=4 * count * width,
    )
    cent_grad, late = call(
        functools.partial(centroid_body, scale),
        [((1, width), F32), mark_shape],
        "svvvvv",
        (sec, logit_first, logit_second, received, low, high),
        flops=4 * rows * width,
        moved=6 * rows * width,
    )
    (grads,) = call(
        finish_body,
        [((count, width), BF16)],
        "svvvvvvvv",
        (sec, own, other, mine, swap(mine), grads_second, grads_other, mark, late),
        flops=2 * rows * count * width,
        moved=4 * rows * width,
    )
    return (acts[None], grads[None], cent_grad[None])


def solution(mesh):
    return jax.shard_map(
        shards,
        mesh=mesh,
        in_specs=(
            P("expert", None),
            P("expert", None),
            P("section", "expert"),
            P("section", "expert", None, None),
            P("section", "expert", None, None),
            P("section", "expert", None),
        ),
        out_specs=(
            P("section", "expert", None),
            P("section", "expert", None),
            P("section", "expert", None),
        ),
        check_vma=False,
    )
```

```python
import functools
import math

import jax
import jax.numpy as jnp
from jax import lax
from jax.experimental import pallas as pl
from jax.experimental.pallas import tpu as pltpu
from jax.sharding import PartitionSpec as P

BF16 = jnp.bfloat16
F32 = jnp.float32
NN = (((1,), (0,)), ((), ()))
NT = (((1,), (1,)), ((), ()))
TN = (((0,), (0,)), ((), ()))
PARTS = 4


def mul(left, right, dims=NN):
    return lax.dot_general(left, right, dims, preferred_element_type=F32)


def call(body, outs, ins, args, scratch=(), flops=0, moved=0, grant=16):
    specs = []
    for kind in ins:
        specs.append(
            pl.BlockSpec(
                memory_space={"s": pltpu.SMEM, "v": pltpu.VMEM, "h": pltpu.HBM}[kind]
            )
        )
    return pl.pallas_call(
        body,
        out_shape=[jax.ShapeDtypeStruct(shape, dtype) for shape, dtype in outs],
        in_specs=specs,
        out_specs=[pl.BlockSpec(memory_space=pltpu.VMEM) for _ in outs],
        scratch_shapes=list(scratch),
        compiler_params=pltpu.CompilerParams(vmem_limit_bytes=grant * 2**20),
        cost_estimate=pl.CostEstimate(flops=flops, bytes_accessed=moved, transcendentals=0),
    )(*args)


def spread_matrix(slot, rows):
    place = lax.broadcasted_iota(jnp.int32, (rows, slot.shape[1]), 0)
    return jnp.where(place == slot, 1.0, 0.0).astype(BF16)


def pick(is_first, first, second):
    return jnp.where(is_first, first, second)


def blocks(total, parts):
    step = total // parts
    return [slice(k * step, (k + 1) * step) for k in range(parts)]


def pack_body(capacity, ids, rows, packed, slot_out):
    count = ids.shape[1]
    across = jnp.broadcast_to(ids[...].astype(F32), (count, count))
    down = across.T
    earlier = lax.broadcasted_iota(jnp.int32, (count, count), 0) < lax.broadcasted_iota(
        jnp.int32, (count, count), 1
    )
    rank = jnp.sum(jnp.where((across == down) & earlier, 1.0, 0.0), axis=0, keepdims=True)
    slot = ids[...] * capacity + rank.astype(jnp.int32)
    slot_out[...] = slot
    packed[...] = mul(spread_matrix(slot, packed.shape[0]), rows[...]).astype(BF16)


def gate_sum(rows, centroid, start):
    total = 0.0
    for at in blocks(rows.shape[1], 4):
        total = total + jnp.sum(
            rows[:, at].astype(F32) * centroid[:, start + at.start : start + at.stop],
            axis=1,
            keepdims=True,
        )
    return total


def spread_column(values, ref):
    ref[...] = jnp.broadcast_to(values, ref.shape)


def first_body(scale, sec, rows, up, down, centroid, send, keep, hidden, aux, gating_out):
    half = send.shape[1]

    @pl.when(sec[0] == 0)
    def _():
        gating = jax.nn.sigmoid(gate_sum(rows, centroid, 0) * scale)
        spread_column(gating, gating_out)
        for at in blocks(up.shape[1], PARTS):
            preact = mul(rows[...], up[:, at])
            sig = jax.nn.sigmoid(preact)
            hidden[:, at] = (preact * sig).astype(BF16)
            aux[:, at] = sig * (1.0 + preact * (1.0 - sig))
        for target, start in ((send, half), (keep, 0)):
            for at in blocks(half, 2):
                into = slice(start + at.start, start + at.stop)
                target[:, at] = (gating * mul(hidden[...], down[:, into])).astype(BF16)

    @pl.when(sec[0] != 0)
    def _():
        for at in blocks(down.shape[0], PARTS):
            aux[:, at] = mul(rows[...], down[at, :], NT)


def choose_body(keeper, sec, keep, arrived, *rest):
    result = rest[-1]

    @pl.when(sec[0] == keeper)
    def _():
        result[...] = keep[...]

    @pl.when(sec[0] != keeper)
    def _():
        result[...] = arrived[...]


def second_ahead_body(sec, high, up, centroid, preact, gate_out):
    half = high.shape[1]

    @pl.when(sec[0] != 0)
    def _():
        spread_column(gate_sum(high, centroid, half), gate_out)
        for at in blocks(up.shape[1], PARTS):
            preact[:, at] = mul(high[...], up[half:, at])


def input_grads(scale, target, start, pre_grad, logit, up, centroid):
    for at in blocks(target.shape[1], 2):
        into = slice(start + at.start, start + at.stop)
        grad = mul(pre_grad[...], up[into, :], NT) + logit * (centroid[:, into] * scale)
        target[:, at] = grad.astype(BF16)


def second_body(
    scale, sec, low, ahead, gate_ahead, back, up, centroid,
    send, logit_out, hidden, pre_grad, gating_out,
):
    half = low.shape[1]

    @pl.when(sec[0] != 0)
    def _():
        gating = jax.nn.sigmoid((gate_sum(low, centroid, 0) + gate_ahead[:, 0:1]) * scale)
        spread_column(gating, gating_out)
        total = 0.0
        for at in blocks(up.shape[1], PARTS):
            preact = mul(low[...], up[:half, at]) + ahead[:, at]
            sig = jax.nn.sigmoid(preact)
            hidden_part = (preact * sig).astype(BF16)
            hidden[:, at] = hidden_part
            back_part = back[:, at]
            total = total + jnp.sum(hidden_part.astype(F32) * back_part, axis=1, keepdims=True)
            slope = sig * (1.0 + preact * (1.0 - sig))
            pre_grad[:, at] = (gating * back_part * slope).astype(BF16)
        logit = total * gating * (1.0 - gating)
        spread_column(logit, logit_out)
        input_grads(scale, send, 0, pre_grad, logit, up, centroid)


def weighted_sum(weight, rows):
    return jnp.sum(weight * rows.astype(F32), axis=0, keepdims=True)


def second_stay_body(scale, sec, logit, pre_grad, up, centroid, low, high, keep, cent):
    half = keep.shape[1]

    @pl.when(sec[0] != 0)
    def _():
        weight = logit[:, 0:1] * scale
        cent[:, :half] = weighted_sum(weight, low[...])
        cent[:, half:] = weighted_sum(weight, high[...])
        input_grads(scale, keep, keep.shape[1], pre_grad, logit[:, 0:1], up, centroid)


def grads_ahead_body(sec, low, down, back):
    half = low.shape[1]

    @pl.when(sec[0] == 0)
    def _():
        for at in blocks(down.shape[0], PARTS):
            back[:, at] = mul(low[...], down[at, :half], NT)


def last_body(
    scale, sec, high, ahead, hidden, slope, gating_in, up, down, centroid,
    hidden_second, gating_second, rows_first, cent_second, grads_other,
    result, cent, pre_grad,
):
    half = high.shape[1]

    @pl.when(sec[0] == 0)
    def _():
        gating = gating_in[:, 0:1]
        total = 0.0
        for at in blocks(down.shape[0], PARTS):
            back = mul(high[...], down[at, half:], NT) + ahead[:, at]
            total = total + jnp.sum(hidden[:, at].astype(F32) * back, axis=1, keepdims=True)
            pre_grad[:, at] = (gating * back * slope[:, at]).astype(BF16)
        logit = total * gating * (1.0 - gating)
        for at in blocks(result.shape[1], PARTS):
            grad = mul(pre_grad[...], up[at, :], NT) + logit * (centroid[:, at] * scale)
            result[:, at] = grad.astype(BF16)
            cent[:, at] = weighted_sum(logit * scale, rows_first[:, at])

    @pl.when(sec[0] != 0)
    def _():
        for at in blocks(result.shape[1], PARTS):
            branch = gating_second[:, 0:1] * mul(hidden_second[...], down[:, at])
            result[:, at] = branch.astype(BF16)
        cent[...] = cent_second[...]


def relay_body(back, sec, own, other, returned, base, result, packed):
    forward = sec[0] == (1 if back else 0)
    slot_from = pick(forward, own[...], other[...])
    slot_to = pick(forward, other[...], own[...])
    rows, width = packed.shape
    mine = pl.ds(pl.multiple_of(sec[0] * width, 128), width)
    change = mul(spread_matrix(slot_from, rows), returned[...], TN)
    result[...] = (base[:, mine].astype(F32) + change).astype(BF16)
    packed[...] = mul(spread_matrix(slot_to, rows), result[...]).astype(BF16)


def finish_body(
    sec, own, returned, acts_mine, acts_other, grads_mine, grads_other, acts, grads
):
    rows = returned.shape[0]
    width = acts_mine.shape[1]
    spread = spread_matrix(own[...], rows)
    acts_parts = (acts_mine, acts_other)
    grads_parts = (grads_mine, grads_other)

    def add(base, at):
        return (base[...].astype(F32) + mul(spread, returned[:, at], TN)).astype(BF16)

    @pl.when(sec[0] == 0)
    def _():
        for k in range(2):
            at = slice(k * width, (k + 1) * width)
            acts[:, at] = acts_parts[k][...]
            grads[:, at] = add(grads_parts[k], at)

    @pl.when(sec[0] != 0)
    def _():
        for k in range(2):
            at = slice(k * width, (k + 1) * width)
            acts[:, at] = add(acts_parts[1 - k], at)
            grads[:, at] = grads_parts[1 - k][...]


def swap(value):
    return lax.ppermute(value, "section", [(0, 1), (1, 0)])


def exchange(value):
    return lax.all_to_all(value, "expert", split_axis=0, concat_axis=0, tiled=True)


def shards(tokens, cotangent, expert_ids, up_weight, down_weight, centroids):
    experts = lax.axis_size("expert")
    count, width = tokens.shape
    hidden_width = up_weight.shape[3]
    half = width // 2
    capacity = 2 * count // experts
    rows = experts * capacity
    scale = 1.0 / math.sqrt(width)
    up = up_weight.reshape(width, hidden_width)
    down = down_weight.reshape(hidden_width, width)
    centroid = centroids.reshape(1, width)
    section = lax.axis_index("section")
    is_first = section == 0
    sec = section.astype(jnp.int32).reshape(1)

    product = 2 * rows * width * hidden_width

    wide, tall, thin = ((rows, width), BF16), ((rows, hidden_width), BF16), ((rows, 128), F32)
    narrow, deep = ((rows, half), BF16), ((rows, hidden_width), F32)
    home = ((count, half), BF16)

    packed, own = call(
        functools.partial(pack_body, capacity),
        [wide, ((1, count), jnp.int32)],
        "vv",
        (expert_ids, jnp.where(is_first, tokens, cotangent)),
        flops=100 * product,
        moved=4 * rows * width,
    )
    received = exchange(packed)
    other = swap(own)

    send, keep, hidden, aux, gating = call(
        functools.partial(first_body, scale),
        [narrow, narrow, tall, deep, thin],
        "svvvv",
        (sec, received, up, down, centroid),
        flops=2 * product,
        moved=10 * rows * width,
    )
    (chosen,) = call(
        functools.partial(choose_body, 0),
        [narrow],
        "svvv",
        (sec, keep, swap(send), other),
        flops=100 * product,
    )
    returned = exchange(chosen)
    acts_first, packed = call(
        functools.partial(relay_body, False),
        [home, narrow],
        "svvvv",
        (sec, own, other, returned, tokens),
        flops=100 * product,
        moved=4 * rows * half + 4 * count * width,
    )

    high = exchange(packed)
    low = swap(high)
    acts_other = swap(acts_first)
    ahead, gate_ahead = call(
        second_ahead_body,
        [deep, thin],
        "svvv",
        (sec, high, up, centroid),
        flops=product // 2,
        moved=4 * rows * width,
    )
    send, logit_second, hidden_second, pre_grad, gating_second = call(
        functools.partial(second_body, scale),
        [narrow, thin, tall, tall, thin],
        "svvvvvv",
        (sec, low, ahead, gate_ahead, aux, up, centroid),
        flops=product,
        moved=10 * rows * width,
    )
    keep, cent_second = call(
        functools.partial(second_stay_body, scale),
        [narrow, ((1, width), F32)],
        "svvvvvv",
        (sec, logit_second, pre_grad, up, centroid, low, high),
        flops=product // 2,
        moved=6 * rows * width,
    )
    (chosen,) = call(
        functools.partial(choose_body, 1),
        [narrow],
        "svvv",
        (sec, keep, swap(send), acts_other),
        flops=100 * product,
    )
    returned = exchange(chosen)
    grads_second, packed = call(
        functools.partial(relay_body, True),
        [home, narrow],
        "svvvv",
        (sec, own, other, returned, cotangent),
        flops=100 * product,
        moved=4 * rows * half + 4 * count * width,
    )

    mine = exchange(packed)
    theirs = swap(mine)
    grads_other = swap(grads_second)
    (ahead,) = call(
        grads_ahead_body,
        [deep],
        "svv",
        (sec, mine, down),
        flops=product // 2,
        moved=4 * rows * width,
    )
    results, cent_grad = call(
        functools.partial(last_body, scale),
        [wide, ((1, width), F32)],
        "svvvvvvvvvvvvv",
        (
            sec, theirs, ahead, hidden, aux, gating, up, down, centroid,
            hidden_second, gating_second, received, cent_second, grads_other,
        ),
        (pltpu.VMEM((rows, hidden_width), BF16),),
        flops=2 * product,
        moved=10 * rows * width,
    )
    returned = exchange(results)
    acts, grads = call(
        finish_body,
        [((count, width), BF16), ((count, width), BF16)],
        "svvvvvv",
        (sec, own, returned, acts_first, acts_other, grads_second, grads_other),
        flops=2 * rows * count * width,
        moved=4 * rows * width,
    )
    return (acts[None], grads[None], cent_grad[None])


def solution(mesh):
    return jax.shard_map(
        shards,
        mesh=mesh,
        in_specs=(
            P("expert", None),
            P("expert", None),
            P("section", "expert"),
            P("section", "expert", None, None),
            P("section", "expert", None, None),
            P("section", "expert", None),
        ),
        out_specs=(
            P("section", "expert", None),
            P("section", "expert", None),
            P("section", "expert", None),
        ),
        check_vma=False,
    )
```

```python
import functools
import math

import jax
import jax.numpy as jnp
from jax import lax
from jax.experimental import pallas as pl
from jax.experimental.pallas import tpu as pltpu
from jax.sharding import PartitionSpec as P

BF16 = jnp.bfloat16
F32 = jnp.float32
NN = (((1,), (0,)), ((), ()))
NT = (((1,), (1,)), ((), ()))
TN = (((0,), (0,)), ((), ()))
PARTS = 2


def mul(left, right, dims=NN):
    return lax.dot_general(left, right, dims, preferred_element_type=F32)


def call(body, outs, ins, args, scratch=(), flops=0, moved=0, grant=16):
    specs = []
    for kind in ins:
        specs.append(
            pl.BlockSpec(
                memory_space={"s": pltpu.SMEM, "v": pltpu.VMEM, "h": pltpu.HBM}[kind]
            )
        )
    return pl.pallas_call(
        body,
        out_shape=[jax.ShapeDtypeStruct(shape, dtype) for shape, dtype in outs],
        in_specs=specs,
        out_specs=[pl.BlockSpec(memory_space=pltpu.VMEM) for _ in outs],
        scratch_shapes=list(scratch),
        compiler_params=pltpu.CompilerParams(vmem_limit_bytes=grant * 2**20),
        cost_estimate=pl.CostEstimate(flops=flops, bytes_accessed=moved, transcendentals=0),
    )(*args)


def spread_matrix(slot, rows):
    place = lax.broadcasted_iota(jnp.int32, (rows, slot.shape[1]), 0)
    return jnp.where(place == slot, 1.0, 0.0).astype(BF16)


def pick(is_first, first, second):
    return jnp.where(is_first, first, second)


def blocks(total, parts):
    step = total // parts
    return [slice(k * step, (k + 1) * step) for k in range(parts)]


def pack_body(capacity, ids, rows, packed, slot_out):
    count = ids.shape[1]
    across = jnp.broadcast_to(ids[...].astype(F32), (count, count))
    down = across.T
    earlier = lax.broadcasted_iota(jnp.int32, (count, count), 0) < lax.broadcasted_iota(
        jnp.int32, (count, count), 1
    )
    rank = jnp.sum(jnp.where((across == down) & earlier, 1.0, 0.0), axis=0, keepdims=True)
    slot = ids[...] * capacity + rank.astype(jnp.int32)
    slot_out[...] = slot
    packed[...] = mul(spread_matrix(slot, packed.shape[0]), rows[...]).astype(BF16)


def gate_sum(rows, centroid, start):
    total = 0.0
    for at in blocks(rows.shape[1], 4):
        total = total + jnp.sum(
            rows[:, at].astype(F32) * centroid[:, start + at.start : start + at.stop],
            axis=1,
            keepdims=True,
        )
    return total


def spread_column(values, ref):
    ref[...] = jnp.broadcast_to(values, ref.shape)


def first_body(scale, sec, rows, up, down, centroid, send, keep, hidden, aux, gating_out):
    half = send.shape[1]

    @pl.when(sec[0] == 0)
    def _():
        gating = jax.nn.sigmoid(gate_sum(rows, centroid, 0) * scale)
        spread_column(gating, gating_out)
        for at in blocks(up.shape[1], PARTS):
            preact = mul(rows[...], up[:, at])
            sig = jax.nn.sigmoid(preact)
            hidden[:, at] = (preact * sig).astype(BF16)
            aux[:, at] = sig * (1.0 + preact * (1.0 - sig))
        for target, start in ((send, half), (keep, 0)):
            for at in blocks(half, 2):
                into = slice(start + at.start, start + at.stop)
                target[:, at] = (gating * mul(hidden[...], down[:, into])).astype(BF16)

    @pl.when(sec[0] != 0)
    def _():
        for at in blocks(down.shape[0], PARTS):
            aux[:, at] = mul(rows[...], down[at, :], NT)


def choose_body(keeper, sec, keep, arrived, *rest):
    result = rest[-1]

    @pl.when(sec[0] == keeper)
    def _():
        result[...] = keep[...]

    @pl.when(sec[0] != keeper)
    def _():
        result[...] = arrived[...]


def second_ahead_body(sec, high, up, centroid, preact, gate_out):
    half = high.shape[1]

    @pl.when(sec[0] != 0)
    def _():
        spread_column(gate_sum(high, centroid, half), gate_out)
        for at in blocks(up.shape[1], PARTS):
            preact[:, at] = mul(high[...], up[half:, at])


def input_grads(scale, target, start, pre_grad, logit, up, centroid):
    for at in blocks(target.shape[1], 2):
        into = slice(start + at.start, start + at.stop)
        grad = mul(pre_grad[...], up[into, :], NT) + logit * (centroid[:, into] * scale)
        target[:, at] = grad.astype(BF16)


def second_body(
    scale, sec, low, ahead, gate_ahead, back, up, centroid,
    send, logit_out, hidden, pre_grad, gating_out,
):
    half = low.shape[1]

    @pl.when(sec[0] != 0)
    def _():
        gating = jax.nn.sigmoid((gate_sum(low, centroid, 0) + gate_ahead[:, 0:1]) * scale)
        spread_column(gating, gating_out)
        total = 0.0
        for at in blocks(up.shape[1], PARTS):
            preact = mul(low[...], up[:half, at]) + ahead[:, at]
            sig = jax.nn.sigmoid(preact)
            hidden_part = (preact * sig).astype(BF16)
            hidden[:, at] = hidden_part
            back_part = back[:, at]
            total = total + jnp.sum(hidden_part.astype(F32) * back_part, axis=1, keepdims=True)
            slope = sig * (1.0 + preact * (1.0 - sig))
            pre_grad[:, at] = (gating * back_part * slope).astype(BF16)
        logit = total * gating * (1.0 - gating)
        spread_column(logit, logit_out)
        input_grads(scale, send, 0, pre_grad, logit, up, centroid)


def weighted_sum(weight, rows):
    return jnp.sum(weight * rows.astype(F32), axis=0, keepdims=True)


def second_stay_body(scale, sec, logit, pre_grad, up, centroid, low, high, keep, cent):
    half = keep.shape[1]

    @pl.when(sec[0] != 0)
    def _():
        weight = logit[:, 0:1] * scale
        cent[:, :half] = weighted_sum(weight, low[...])
        cent[:, half:] = weighted_sum(weight, high[...])
        input_grads(scale, keep, keep.shape[1], pre_grad, logit[:, 0:1], up, centroid)


def grads_ahead_body(sec, low, down, back):
    half = low.shape[1]

    @pl.when(sec[0] == 0)
    def _():
        for at in blocks(down.shape[0], PARTS):
            back[:, at] = mul(low[...], down[at, :half], NT)


def last_body(
    scale, sec, high, ahead, hidden, slope, gating_in, up, down, centroid,
    hidden_second, gating_second, rows_first, cent_second, grads_other,
    result, cent, pre_grad,
):
    half = high.shape[1]

    @pl.when(sec[0] == 0)
    def _():
        gating = gating_in[:, 0:1]
        total = 0.0
        for at in blocks(down.shape[0], PARTS):
            back = mul(high[...], down[at, half:], NT) + ahead[:, at]
            total = total + jnp.sum(hidden[:, at].astype(F32) * back, axis=1, keepdims=True)
            pre_grad[:, at] = (gating * back * slope[:, at]).astype(BF16)
        logit = total * gating * (1.0 - gating)
        for at in blocks(result.shape[1], PARTS):
            grad = mul(pre_grad[...], up[at, :], NT) + logit * (centroid[:, at] * scale)
            result[:, at] = grad.astype(BF16)
            cent[:, at] = weighted_sum(logit * scale, rows_first[:, at])

    @pl.when(sec[0] != 0)
    def _():
        for at in blocks(result.shape[1], PARTS):
            branch = gating_second[:, 0:1] * mul(hidden_second[...], down[:, at])
            result[:, at] = branch.astype(BF16)
        cent[...] = cent_second[...]


def relay_body(back, sec, own, other, returned, base, result, packed):
    forward = sec[0] == (1 if back else 0)
    slot_from = pick(forward, own[...], other[...])
    slot_to = pick(forward, other[...], own[...])
    rows, width = packed.shape
    mine = pl.ds(pl.multiple_of(sec[0] * width, 128), width)
    change = mul(spread_matrix(slot_from, rows), returned[...], TN)
    result[...] = (base[:, mine].astype(F32) + change).astype(BF16)
    packed[...] = mul(spread_matrix(slot_to, rows), result[...]).astype(BF16)


def finish_body(
    sec, own, returned, acts_mine, acts_other, grads_mine, grads_other, acts, grads
):
    rows = returned.shape[0]
    width = acts_mine.shape[1]
    spread = spread_matrix(own[...], rows)
    acts_parts = (acts_mine, acts_other)
    grads_parts = (grads_mine, grads_other)

    def add(base, at):
        return (base[...].astype(F32) + mul(spread, returned[:, at], TN)).astype(BF16)

    @pl.when(sec[0] == 0)
    def _():
        for k in range(2):
            at = slice(k * width, (k + 1) * width)
            acts[:, at] = acts_parts[k][...]
            grads[:, at] = add(grads_parts[k], at)

    @pl.when(sec[0] != 0)
    def _():
        for k in range(2):
            at = slice(k * width, (k + 1) * width)
            acts[:, at] = add(acts_parts[1 - k], at)
            grads[:, at] = grads_parts[1 - k][...]


def swap(value):
    return lax.ppermute(value, "section", [(0, 1), (1, 0)])


def exchange(value):
    return lax.all_to_all(value, "expert", split_axis=0, concat_axis=0, tiled=True)


def shards(tokens, cotangent, expert_ids, up_weight, down_weight, centroids):
    experts = lax.axis_size("expert")
    count, width = tokens.shape
    hidden_width = up_weight.shape[3]
    half = width // 2
    capacity = 2 * count // experts
    rows = experts * capacity
    scale = 1.0 / math.sqrt(width)
    up = up_weight.reshape(width, hidden_width)
    down = down_weight.reshape(hidden_width, width)
    centroid = centroids.reshape(1, width)
    section = lax.axis_index("section")
    is_first = section == 0
    sec = section.astype(jnp.int32).reshape(1)

    product = 2 * rows * width * hidden_width

    wide, tall, thin = ((rows, width), BF16), ((rows, hidden_width), BF16), ((rows, 128), F32)
    narrow, deep = ((rows, half), BF16), ((rows, hidden_width), F32)
    home = ((count, half), BF16)

    packed, own = call(
        functools.partial(pack_body, capacity),
        [wide, ((1, count), jnp.int32)],
        "vv",
        (expert_ids, jnp.where(is_first, tokens, cotangent)),
        flops=100 * product,
        moved=4 * rows * width,
    )
    received = exchange(packed)
    other = swap(own)

    send, keep, hidden, aux, gating = call(
        functools.partial(first_body, scale),
        [narrow, narrow, tall, deep, thin],
        "svvvv",
        (sec, received, up, down, centroid),
        flops=2 * product,
        moved=10 * rows * width,
    )
    (chosen,) = call(
        functools.partial(choose_body, 0),
        [narrow],
        "svvv",
        (sec, keep, swap(send), other),
        flops=100 * product,
    )
    returned = exchange(chosen)
    acts_first, packed = call(
        functools.partial(relay_body, False),
        [home, narrow],
        "svvvv",
        (sec, own, other, returned, tokens),
        flops=100 * product,
        moved=4 * rows * half + 4 * count * width,
    )

    high = exchange(packed)
    low = swap(high)
    acts_other = swap(acts_first)
    ahead, gate_ahead = call(
        second_ahead_body,
        [deep, thin],
        "svvv",
        (sec, high, up, centroid),
        flops=product // 2,
        moved=4 * rows * width,
    )
    send, logit_second, hidden_second, pre_grad, gating_second = call(
        functools.partial(second_body, scale),
        [narrow, thin, tall, tall, thin],
        "svvvvvv",
        (sec, low, ahead, gate_ahead, aux, up, centroid),
        flops=product,
        moved=10 * rows * width,
    )
    keep, cent_second = call(
        functools.partial(second_stay_body, scale),
        [narrow, ((1, width), F32)],
        "svvvvvv",
        (sec, logit_second, pre_grad, up, centroid, low, high),
        flops=product // 2,
        moved=6 * rows * width,
    )
    (chosen,) = call(
        functools.partial(choose_body, 1),
        [narrow],
        "svvv",
        (sec, keep, swap(send), acts_other),
        flops=100 * product,
    )
    returned = exchange(chosen)
    grads_second, packed = call(
        functools.partial(relay_body, True),
        [home, narrow],
        "svvvv",
        (sec, own, other, returned, cotangent),
        flops=100 * product,
        moved=4 * rows * half + 4 * count * width,
    )

    mine = exchange(packed)
    theirs = swap(mine)
    grads_other = swap(grads_second)
    (ahead,) = call(
        grads_ahead_body,
        [deep],
        "svv",
        (sec, mine, down),
        flops=product // 2,
        moved=4 * rows * width,
    )
    results, cent_grad = call(
        functools.partial(last_body, scale),
        [wide, ((1, width), F32)],
        "svvvvvvvvvvvvv",
        (
            sec, theirs, ahead, hidden, aux, gating, up, down, centroid,
            hidden_second, gating_second, received, cent_second, grads_other,
        ),
        (pltpu.VMEM((rows, hidden_width), BF16),),
        flops=2 * product,
        moved=10 * rows * width,
    )
    returned = exchange(results)
    acts, grads = call(
        finish_body,
        [((count, width), BF16), ((count, width), BF16)],
        "svvvvvv",
        (sec, own, returned, acts_first, acts_other, grads_second, grads_other),
        flops=2 * rows * count * width,
        moved=4 * rows * width,
    )
    return (acts[None], grads[None], cent_grad[None])


def solution(mesh):
    return jax.shard_map(
        shards,
        mesh=mesh,
        in_specs=(
            P("expert", None),
            P("expert", None),
            P("section", "expert"),
            P("section", "expert", None, None),
            P("section", "expert", None, None),
            P("section", "expert", None),
        ),
        out_specs=(
            P("section", "expert", None),
            P("section", "expert", None),
            P("section", "expert", None),
        ),
        check_vma=False,
    )
```

```python
import functools
import math

import jax
import jax.numpy as jnp
from jax import lax
from jax.experimental import pallas as pl
from jax.experimental.pallas import tpu as pltpu
from jax.sharding import PartitionSpec as P

BF16 = jnp.bfloat16
F32 = jnp.float32
NN = (((1,), (0,)), ((), ()))
NT = (((1,), (1,)), ((), ()))
TN = (((0,), (0,)), ((), ()))
PARTS = 2


def mul(left, right, dims=NN):
    return lax.dot_general(left, right, dims, preferred_element_type=F32)


def call(body, outs, ins, args, scratch=(), flops=0, moved=0, grant=16):
    specs = []
    for kind in ins:
        specs.append(
            pl.BlockSpec(
                memory_space={"s": pltpu.SMEM, "v": pltpu.VMEM, "h": pltpu.HBM}[kind]
            )
        )
    return pl.pallas_call(
        body,
        out_shape=[jax.ShapeDtypeStruct(shape, dtype) for shape, dtype in outs],
        in_specs=specs,
        out_specs=[pl.BlockSpec(memory_space=pltpu.VMEM) for _ in outs],
        scratch_shapes=list(scratch),
        compiler_params=pltpu.CompilerParams(vmem_limit_bytes=grant * 2**20),
        cost_estimate=pl.CostEstimate(flops=flops, bytes_accessed=moved, transcendentals=0),
    )(*args)


def spread_matrix(slot, rows):
    place = lax.broadcasted_iota(jnp.int32, (rows, slot.shape[1]), 0)
    return jnp.where(place == slot, 1.0, 0.0).astype(BF16)


def pick(is_first, first, second):
    return jnp.where(is_first, first, second)


def blocks(total, parts):
    step = total // parts
    return [slice(k * step, (k + 1) * step) for k in range(parts)]


def pack_body(capacity, ids, rows, packed, slot_out):
    count = ids.shape[1]
    across = jnp.broadcast_to(ids[...].astype(F32), (count, count))
    down = across.T
    earlier = lax.broadcasted_iota(jnp.int32, (count, count), 0) < lax.broadcasted_iota(
        jnp.int32, (count, count), 1
    )
    rank = jnp.sum(jnp.where((across == down) & earlier, 1.0, 0.0), axis=0, keepdims=True)
    slot = ids[...] * capacity + rank.astype(jnp.int32)
    slot_out[...] = slot
    packed[...] = mul(spread_matrix(slot, packed.shape[0]), rows[...]).astype(BF16)


def gate_sum(rows, centroid, start):
    total = 0.0
    for at in blocks(rows.shape[1], 4):
        total = total + jnp.sum(
            rows[:, at].astype(F32) * centroid[:, start + at.start : start + at.stop],
            axis=1,
            keepdims=True,
        )
    return total


def spread_column(values, ref):
    ref[...] = jnp.broadcast_to(values, ref.shape)


def first_body(scale, sec, rows, up, down, centroid, send, keep, hidden, aux, gating_out):
    half = send.shape[1]

    @pl.when(sec[0] == 0)
    def _():
        gating = jax.nn.sigmoid(gate_sum(rows, centroid, 0) * scale)
        spread_column(gating, gating_out)
        for at in blocks(up.shape[1], PARTS):
            preact = mul(rows[...], up[:, at])
            sig = jax.nn.sigmoid(preact)
            hidden[:, at] = (preact * sig).astype(BF16)
            aux[:, at] = sig * (1.0 + preact * (1.0 - sig))
        for target, start in ((send, half), (keep, 0)):
            for at in blocks(half, 2):
                into = slice(start + at.start, start + at.stop)
                target[:, at] = (gating * mul(hidden[...], down[:, into])).astype(BF16)

    @pl.when(sec[0] != 0)
    def _():
        for at in blocks(down.shape[0], PARTS):
            aux[:, at] = mul(rows[...], down[at, :], NT)


def choose_body(keeper, sec, keep, arrived, *rest):
    result = rest[-1]

    @pl.when(sec[0] == keeper)
    def _():
        result[...] = keep[...]

    @pl.when(sec[0] != keeper)
    def _():
        result[...] = arrived[...]


def second_ahead_body(sec, high, up, centroid, preact, gate_out):
    half = high.shape[1]

    @pl.when(sec[0] != 0)
    def _():
        spread_column(gate_sum(high, centroid, half), gate_out)
        for at in blocks(up.shape[1], PARTS):
            preact[:, at] = mul(high[...], up[half:, at])


def input_grads(scale, target, start, pre_grad, logit, up, centroid):
    for at in blocks(target.shape[1], 2):
        into = slice(start + at.start, start + at.stop)
        grad = mul(pre_grad[...], up[into, :], NT) + logit * (centroid[:, into] * scale)
        target[:, at] = grad.astype(BF16)


def second_body(
    scale, sec, low, ahead, gate_ahead, back, up, centroid,
    send, logit_out, hidden, pre_grad, gating_out,
):
    half = low.shape[1]

    @pl.when(sec[0] != 0)
    def _():
        gating = jax.nn.sigmoid((gate_sum(low, centroid, 0) + gate_ahead[:, 0:1]) * scale)
        spread_column(gating, gating_out)
        total = 0.0
        for at in blocks(up.shape[1], PARTS):
            preact = mul(low[...], up[:half, at]) + ahead[:, at]
            sig = jax.nn.sigmoid(preact)
            hidden_part = (preact * sig).astype(BF16)
            hidden[:, at] = hidden_part
            back_part = back[:, at]
            total = total + jnp.sum(hidden_part.astype(F32) * back_part, axis=1, keepdims=True)
            slope = sig * (1.0 + preact * (1.0 - sig))
            pre_grad[:, at] = (gating * back_part * slope).astype(BF16)
        logit = total * gating * (1.0 - gating)
        spread_column(logit, logit_out)
        input_grads(scale, send, 0, pre_grad, logit, up, centroid)


def weighted_sum(weight, rows):
    return jnp.sum(weight * rows.astype(F32), axis=0, keepdims=True)


def second_stay_body(scale, sec, logit, pre_grad, up, centroid, low, high, keep, cent):
    half = keep.shape[1]

    @pl.when(sec[0] != 0)
    def _():
        weight = logit[:, 0:1] * scale
        cent[:, :half] = weighted_sum(weight, low[...])
        cent[:, half:] = weighted_sum(weight, high[...])
        input_grads(scale, keep, keep.shape[1], pre_grad, logit[:, 0:1], up, centroid)


def grads_ahead_body(sec, low, down, back):
    half = low.shape[1]

    @pl.when(sec[0] == 0)
    def _():
        for at in blocks(down.shape[0], PARTS):
            back[:, at] = mul(low[...], down[at, :half], NT)


def last_body(
    scale, sec, high, ahead, hidden, slope, gating_in, up, down, centroid,
    hidden_second, gating_second, rows_first, cent_second, grads_other,
    result, cent, pre_grad,
):
    half = high.shape[1]

    @pl.when(sec[0] == 0)
    def _():
        gating = gating_in[:, 0:1]
        total = 0.0
        for at in blocks(down.shape[0], PARTS):
            back = mul(high[...], down[at, half:], NT) + ahead[:, at]
            total = total + jnp.sum(hidden[:, at].astype(F32) * back, axis=1, keepdims=True)
            pre_grad[:, at] = (gating * back * slope[:, at]).astype(BF16)
        logit = total * gating * (1.0 - gating)
        for at in blocks(result.shape[1], PARTS):
            grad = mul(pre_grad[...], up[at, :], NT) + logit * (centroid[:, at] * scale)
            result[:, at] = grad.astype(BF16)
            cent[:, at] = weighted_sum(logit * scale, rows_first[:, at])

    @pl.when(sec[0] != 0)
    def _():
        for at in blocks(result.shape[1], PARTS):
            branch = gating_second[:, 0:1] * mul(hidden_second[...], down[:, at])
            result[:, at] = branch.astype(BF16)
        cent[...] = cent_second[...]


def relay_body(back, sec, own, other, returned, base, result, packed):
    forward = sec[0] == (1 if back else 0)
    slot_from = pick(forward, own[...], other[...])
    slot_to = pick(forward, other[...], own[...])
    rows, width = packed.shape
    mine = pl.ds(pl.multiple_of(sec[0] * width, 128), width)
    change = mul(spread_matrix(slot_from, rows), returned[...], TN)
    result[...] = (base[:, mine].astype(F32) + change).astype(BF16)
    packed[...] = mul(spread_matrix(slot_to, rows), result[...]).astype(BF16)


def finish_body(
    sec, own, returned, acts_mine, acts_other, grads_mine, grads_other, acts, grads
):
    rows = returned.shape[0]
    width = acts_mine.shape[1]
    spread = spread_matrix(own[...], rows)
    acts_parts = (acts_mine, acts_other)
    grads_parts = (grads_mine, grads_other)

    def add(base, at):
        return (base[...].astype(F32) + mul(spread, returned[:, at], TN)).astype(BF16)

    @pl.when(sec[0] == 0)
    def _():
        for k in range(2):
            at = slice(k * width, (k + 1) * width)
            acts[:, at] = acts_parts[k][...]
            grads[:, at] = add(grads_parts[k], at)

    @pl.when(sec[0] != 0)
    def _():
        for k in range(2):
            at = slice(k * width, (k + 1) * width)
            acts[:, at] = add(acts_parts[1 - k], at)
            grads[:, at] = grads_parts[1 - k][...]


def swap(value):
    return lax.ppermute(value, "section", [(0, 1), (1, 0)])


def exchange(value):
    return lax.all_to_all(value, "expert", split_axis=0, concat_axis=0, tiled=True)


def shards(tokens, cotangent, expert_ids, up_weight, down_weight, centroids):
    experts = lax.axis_size("expert")
    count, width = tokens.shape
    hidden_width = up_weight.shape[3]
    half = width // 2
    capacity = 2 * count // experts
    rows = experts * capacity
    scale = 1.0 / math.sqrt(width)
    up = up_weight.reshape(width, hidden_width)
    down = down_weight.reshape(hidden_width, width)
    centroid = centroids.reshape(1, width)
    section = lax.axis_index("section")
    is_first = section == 0
    sec = section.astype(jnp.int32).reshape(1)

    product = 2 * rows * width * hidden_width

    wide, tall, thin = ((rows, width), BF16), ((rows, hidden_width), BF16), ((rows, 128), F32)
    narrow, deep = ((rows, half), BF16), ((rows, hidden_width), F32)
    home = ((count, half), BF16)

    packed, own = call(
        functools.partial(pack_body, capacity),
        [wide, ((1, count), jnp.int32)],
        "vv",
        (expert_ids, jnp.where(is_first, tokens, cotangent)),
        flops=100 * product,
        moved=4 * rows * width,
    )
    received = exchange(packed)
    other = swap(own)

    send, keep, hidden, aux, gating = call(
        functools.partial(first_body, scale),
        [narrow, narrow, tall, deep, thin],
        "svvvv",
        (sec, received, up, down, centroid),
        flops=2 * product,
        moved=10 * rows * width,
    )
    (chosen,) = call(
        functools.partial(choose_body, 0),
        [narrow],
        "svvv",
        (sec, keep, swap(send), other),
        flops=100 * product,
    )
    returned = exchange(chosen)
    acts_first, packed = call(
        functools.partial(relay_body, False),
        [home, narrow],
        "svvvv",
        (sec, own, other, returned, tokens),
        flops=100 * product,
        moved=4 * rows * half + 4 * count * width,
    )

    high = exchange(packed)
    low = swap(high)
    ahead, gate_ahead = call(
        second_ahead_body,
        [deep, thin],
        "svvv",
        (sec, high, up, centroid),
        flops=product // 2,
        moved=4 * rows * width,
    )
    send, logit_second, hidden_second, pre_grad, gating_second = call(
        functools.partial(second_body, scale),
        [narrow, thin, tall, tall, thin],
        "svvvvvv",
        (sec, low, ahead, gate_ahead, aux, up, centroid),
        flops=product,
        moved=10 * rows * width,
    )
    keep, cent_second = call(
        functools.partial(second_stay_body, scale),
        [narrow, ((1, width), F32)],
        "svvvvvv",
        (sec, logit_second, pre_grad, up, centroid, low, high),
        flops=product // 2,
        moved=6 * rows * width,
    )
    arrived = swap(send)
    acts_other = swap(acts_first)
    (chosen,) = call(
        functools.partial(choose_body, 1),
        [narrow],
        "svvv",
        (sec, keep, arrived, acts_other),
        flops=100 * product,
    )
    returned = exchange(chosen)
    grads_second, packed = call(
        functools.partial(relay_body, True),
        [home, narrow],
        "svvvv",
        (sec, own, other, returned, cotangent),
        flops=100 * product,
        moved=4 * rows * half + 4 * count * width,
    )

    mine = exchange(packed)
    theirs = swap(mine)
    grads_other = swap(grads_second)
    (ahead,) = call(
        grads_ahead_body,
        [deep],
        "svv",
        (sec, mine, down),
        flops=product // 2,
        moved=4 * rows * width,
    )
    results, cent_grad = call(
        functools.partial(last_body, scale),
        [wide, ((1, width), F32)],
        "svvvvvvvvvvvvv",
        (
            sec, theirs, ahead, hidden, aux, gating, up, down, centroid,
            hidden_second, gating_second, received, cent_second, grads_other,
        ),
        (pltpu.VMEM((rows, hidden_width), BF16),),
        flops=2 * product,
        moved=10 * rows * width,
    )
    returned = exchange(results)
    acts, grads = call(
        finish_body,
        [((count, width), BF16), ((count, width), BF16)],
        "svvvvvv",
        (sec, own, returned, acts_first, acts_other, grads_second, grads_other),
        flops=2 * rows * count * width,
        moved=4 * rows * width,
    )
    return (acts[None], grads[None], cent_grad[None])


def solution(mesh):
    return jax.shard_map(
        shards,
        mesh=mesh,
        in_specs=(
            P("expert", None),
            P("expert", None),
            P("section", "expert"),
            P("section", "expert", None, None),
            P("section", "expert", None, None),
            P("section", "expert", None),
        ),
        out_specs=(
            P("section", "expert", None),
            P("section", "expert", None),
            P("section", "expert", None),
        ),
        check_vma=False,
    )
```
